32 devices in a mesh: group: 2 (over y), ep: 4 (over z), tp: 2 (over x), dp: 2 (over core).
Axes of the slice: x: 2, y: 2, z: 4, core: 2. Of those that a mesh axis runs over, the one named last changes fastest.
Arguments:
- hidden: bfloat16 [256, 7168], P(('group', 'ep', 'dp')), parts along dimension 0, may hold values from -1600 to 1600
- embedded: bfloat16 [256, 7168], P(('group', 'ep', 'dp')), parts along dimension 0, may hold values from -1600 to 1600
- hidden_gain: float32 [7168], replicated, may hold values from 0.1 to 1.9
- embed_gain: float32 [7168], replicated, may hold values from 0.1 to 1.9
- w_embed: bfloat16 [7168, 7168], P(('ep', 'dp'), 'tp'), may hold values from -0.046875 to 0.046875
- w_hidden: bfloat16 [7168, 7168], P(('ep', 'dp'), 'tp'), may hold values from -0.046875 to 0.046875
- w_latent: bfloat16 [7168, 576], P('tp'), may hold values from -0.0625 to 0.0625
- latent_gain: float32 [512], replicated, may hold values from 0.1 to 1.9
- absorbed_query: bfloat16 [256, 128, 576], P(('group', 'ep', 'dp'), 'tp'), parts along dimension 0, may hold values from -49 to 49
- latent_cache: bfloat16 [64, 512, 576], P(('group', 'ep', 'dp')), parts along dimension 0, may hold values from -4.1 to 4.1
- cache_length: int32 [64], P(('group', 'ep', 'dp')), parts along dimension 0, may hold values from 2 to 512, as said below
- expert_ids: int32 [256, 8], P(('group', 'ep', 'dp')), parts along dimension 0, may hold values from 0 to 15, all different within a row; in each aligned block of 16 rows (0 to 15, 16 to 31, ...) at most 12 rows name the same one
- gate_weights: float32 [256, 8], P(('group', 'ep', 'dp')), parts along dimension 0, may hold values from 0.1 to 0.5
- w_gate: bfloat16 [16, 7168, 1024], P('ep', None, ('tp', 'dp')), may hold values from -0.0625 to 0.0625
- w_up: bfloat16 [16, 7168, 1024], P('ep', None, ('tp', 'dp')), may hold values from -0.0625 to 0.0625
- w_down: bfloat16 [16, 1024, 7168], P('ep', ('tp', 'dp')), may hold values from -0.1875 to 0.1875
Outputs:
- latent_attention: bfloat16 [256, 128, 512], P(('group', 'ep', 'dp'), 'tp'), parts along dimension 0
- expert_mix: bfloat16 [256, 7168], P(('group', 'ep', 'dp'), 'tp'), parts along dimension 0
The draws below stay inside these ranges and needn't reach their ends.
There are 2 independent parts, one for each index of `group`. The reference program is written for one: setup_inputs(seed, part) draws one part's arguments, and reference() takes and returns one part's arrays. A program takes and returns all parts, laid end to end along the dimension named above; an argument that names none is the same for every part. Nothing has to cross between parts.
Inputs may be any that keep to these rules, and one draw needn't show every extreme that they name: `expert_ids`: each row names 8 different experts; among the rows of one device no expert is named by more than 12 rows, a bound that some block of them reaches. `cache_length`: some request has all 512 positions in use.
All inputs are finite; a program needn't handle non-finite values.
Results may differ from the reference program's by a relative error of at most 0.025.
Values may be sent and summed in bfloat16 or wider, within the bound.
A program may use at most 192 MiB of HBM per device.

```python
import math
import jax
import jax.numpy as jnp
import numpy as np
from jax import lax

D = 7168
HEADS = 128
LATENT = 512
ROPE = 64
QK_DIM = 192
FF_EXP = 1024
TOP = 8
DRAFTS = 4
CAP = 12
CACHE = 512
EXPERTS = 16
ROWS_DEV = 16
REQS = 32
ROWS = 128
N_EP = 4
N_TP = 2
N_DP = 2


def spread_scales(key, rise_factor):
    key_row, key_column = jax.random.split(key)
    row_scale = jnp.exp(jax.random.uniform(key_row, (ROWS, 1), jnp.float32) * math.log(10.0))
    column_scale = jnp.exp(jax.random.uniform(key_column, (1, D), jnp.float32) * math.log(10.0))
    position_share = jnp.arange(D, dtype=jnp.float32)[None, :] / D
    return row_scale * column_scale * jnp.exp(position_share * math.log(rise_factor))


def cache_base(key):
    return jnp.clip(jax.random.normal(key, (REQS, CACHE, LATENT + ROPE), jnp.float32), -4.0, 4.0)


def draw_hidden(key, part):
    key = jax.random.fold_in(key, 1)
    key_base, key_scale = jax.random.split(key)
    base_values = jnp.clip(jax.random.normal(key_base, (ROWS, D), jnp.float32), -4.0, 4.0)
    return (base_values * spread_scales(key_scale, 3.0)).astype(jnp.bfloat16)


def draw_embedded(key, part):
    key = jax.random.fold_in(key, 2)
    key_base, key_scale = jax.random.split(key)
    base_values = jnp.clip(jax.random.normal(key_base, (ROWS, D), jnp.float32), -4.0, 4.0)
    return (base_values * spread_scales(key_scale, 3.0)).astype(jnp.bfloat16)


def draw_latent_cache(key, part):
    base_values = cache_base(key)
    return base_values.astype(jnp.bfloat16)


def draw_absorbed_query(key, part):
    key = jax.random.fold_in(key, 5)
    key_query = jax.random.fold_in(key, 0)
    return jnp.clip(jax.random.normal(key_query, (ROWS, HEADS, LATENT + ROPE), jnp.float32), -4.0, 4.0).astype(jnp.bfloat16)


def draw_cache_length(key, part):
    key = jax.random.fold_in(key, 7)
    key_length, key_longest = jax.random.split(key)
    lengths = jax.random.randint(key_length, (REQS,), 2, CACHE + 1)
    longest = jax.random.randint(key_longest, (), 0, REQS)
    return jnp.where(jnp.arange(REQS) == longest, CACHE, lengths).astype(jnp.int32)


def level_of(stream_key, extent, shards, least, top_value):
    loudness, own = 1.0, jax.random.fold_in(stream_key, 6)
    for axis_at, parts in shards:
        heights = jnp.exp(jax.random.uniform(jax.random.fold_in(own, axis_at), (parts,), jnp.float32, least / len(shards), top_value / len(shards)))
        loudness = loudness * jnp.repeat(heights, extent[axis_at] // parts).reshape([-1 if axis == axis_at else 1 for axis in range(len(extent))])
    return loudness


def deal_out(key, own, number, rows, count, top, most, skew):
    order = jax.random.permutation(key, count)
    crowded, usual = portions_of(count, rows * top, most, skew, True), portions_of(count, rows * top, most, skew, False)
    places = jnp.arange(count)

    def named(tallies, rotation):
        used = int((tallies > 0).sum())
        fixed = max(1, used // 4)
        shifted = fixed + (places - fixed + rotation * (used - fixed)) % max(1, count - fixed)
        return jnp.zeros((count,), jnp.int32).at[order[jnp.where(places < fixed, places, shifted)]].set(jnp.asarray(tallies, jnp.int32))

    tallies = jnp.where(number % 4 == 0, named(crowded, number // 4), named(usual, number - number // 4 - 1))
    mixed = jax.random.permutation(jax.random.fold_in(own, 3), count)
    giver, receiver = mixed[0:count // 2 * 2:2], mixed[1:count // 2 * 2:2]
    room = jnp.minimum(tallies[giver] - 1, most - tallies[receiver]) // 2
    room = jnp.where((giver == order[0]) | (receiver == order[0]) | (tallies[receiver] == 0), 0, jnp.maximum(room, 0))
    shifted = jax.random.randint(jax.random.fold_in(own, 4), (count // 2,), 0, 1 << 20) % (room + 1)
    tallies = tallies.at[giver].add(-shifted).at[receiver].add(shifted)
    members = jnp.searchsorted(jnp.cumsum(tallies), jnp.arange(rows * top), side="right").astype(jnp.int32)
    table = members.reshape(top, rows).T
    table = table[jax.random.permutation(jax.random.fold_in(own, 1), rows)]
    rotation = jax.random.randint(jax.random.fold_in(own, 2), (rows, 1), 0, top)
    return jnp.take_along_axis(table, (jnp.arange(top)[None, :] + rotation) % top, axis=1)


def portions_of(count, total, limit, skew, full):
    loads = [(1 << 20) // math.isqrt(rank ** skew) + 1 for rank in range(1, count + 1)]
    largest = limit if full else min(limit, max(-(-total // count), total * loads[0] // sum(loads)))
    least = 1 if total - largest >= count - 1 else 0
    holding, spare = [largest] + [least] * (count - 1), total - largest - least * (count - 1)
    while spare > 0:
        candidates = [i for i in range(1, count) if holding[i] < largest] or [i for i in range(1, count) if holding[i] < limit]
        whole, remaining = sum([loads[i] for i in candidates]), spare
        for i in candidates:
            addition = min(limit - holding[i], max(1, remaining * loads[i] // whole), spare)
            holding[i] = holding[i] + addition
            spare = spare - addition
    return np.array(holding)


def bell_draw(rng, extent, width, limit, cuts=(), kind=jnp.bfloat16):
    level = level_of(rng, extent, cuts, -0.22, 0.18) if cuts else 1.0
    values = jax.random.normal(rng, extent, jnp.float32) * width * level
    return jnp.minimum(jnp.maximum(values, -limit), limit).astype(kind)


def setup_inputs(seed: int = 0, part: int = 0) -> dict:
    streams_of = jax.random.split(jax.random.key(seed), 17)
    part_keys = jax.random.split(jax.random.fold_in(streams_of[16], part), 17)
    hidden = draw_hidden(jax.random.fold_in(jax.random.fold_in(streams_of[16], part), 71), part)
    embedded = draw_embedded(jax.random.fold_in(jax.random.fold_in(streams_of[16], part), 71), part)
    hidden_gain = jnp.clip(1.0 + 0.18 * jax.random.normal(streams_of[2], (D,), jnp.float32), 0.1, 1.9)
    embed_gain = jnp.clip(1.0 + 0.18 * jax.random.normal(streams_of[3], (D,), jnp.float32), 0.1, 1.9)
    w_embed = bell_draw(streams_of[4], (D, D), (2 * D) ** -0.5, 0.046875, ((0, 8), (1, 2)))
    w_hidden = bell_draw(streams_of[5], (D, D), (2 * D) ** -0.5, 0.046875, ((0, 8), (1, 2)))
    w_latent = bell_draw(streams_of[6], (D, LATENT + ROPE), D ** -0.5, 0.0625, ((0, 2),))
    latent_gain = jnp.clip(1.0 + 0.18 * jax.random.normal(streams_of[7], (LATENT,), jnp.float32), 0.1, 1.9)
    absorbed_query = draw_absorbed_query(jax.random.fold_in(jax.random.fold_in(streams_of[16], part), 71), part)
    latent_cache = draw_latent_cache(jax.random.fold_in(jax.random.fold_in(streams_of[16], part), 71), part)
    cache_length = draw_cache_length(jax.random.fold_in(jax.random.fold_in(streams_of[16], part), 71), part)
    expert_ids_keys = jax.random.split(jax.random.fold_in(part_keys[11], 1), ROWS // ROWS_DEV)
    expert_ids_turns = jax.random.permutation(jax.random.fold_in(part_keys[11], 3), ROWS // ROWS_DEV)
    expert_ids = jax.vmap(lambda own, number: deal_out(jax.random.fold_in(part_keys[11], 2), own, number, ROWS_DEV, EXPERTS, TOP, CAP, 2))(expert_ids_keys, expert_ids_turns).reshape((ROWS, TOP))
    gate_weights = jnp.clip(0.1 + 0.4 * jax.random.uniform(part_keys[12], (ROWS, TOP), jnp.float32) ** level_of(part_keys[12], (ROWS, TOP), ((0, 8),), -0.2, 0.2), 0.1, 0.5)
    w_gate = bell_draw(streams_of[13], (EXPERTS, D, FF_EXP), D ** -0.5, 0.0625, ((0, 4), (2, 4)))
    w_up = bell_draw(streams_of[14], (EXPERTS, D, FF_EXP), D ** -0.5, 0.0625, ((0, 4), (2, 4)))
    w_down = bell_draw(streams_of[15], (EXPERTS, FF_EXP, D), FF_EXP ** -0.5, 0.1875, ((0, 4), (1, 4)))
    return {"hidden": hidden, "embedded": embedded, "hidden_gain": hidden_gain, "embed_gain": embed_gain, "w_embed": w_embed, "w_hidden": w_hidden, "w_latent": w_latent, "latent_gain": latent_gain, "absorbed_query": absorbed_query, "latent_cache": latent_cache, "cache_length": cache_length, "expert_ids": expert_ids, "gate_weights": gate_weights, "w_gate": w_gate, "w_up": w_up, "w_down": w_down}


EPS = 1e-06

def rms_scale(values, gain_vector):
    wide = values.astype(jnp.float32)
    mean_square = lax.optimization_barrier(jnp.mean(wide * wide, axis=-1, keepdims=True))
    return (wide * lax.rsqrt(mean_square + EPS) * gain_vector.astype(jnp.float32)).astype(jnp.bfloat16)

def reference(hidden, embedded, hidden_gain, embed_gain, w_embed, w_hidden, w_latent, latent_gain, absorbed_query, latent_cache, cache_length, expert_ids, gate_weights, w_gate, w_up, w_down):
    embed_norm = rms_scale(embedded, embed_gain)
    hidden_norm = rms_scale(hidden, hidden_gain)
    projected = (jnp.dot(embed_norm, w_embed, preferred_element_type=jnp.float32) + jnp.dot(hidden_norm, w_hidden, preferred_element_type=jnp.float32)).astype(jnp.bfloat16)
    latent_full = jnp.dot(projected, w_latent, preferred_element_type=jnp.float32)
    new_key = jnp.concatenate([rms_scale(latent_full[:, :LATENT], latent_gain), latent_full[:, LATENT:].astype(jnp.bfloat16)], axis=1)
    score_scale = 1.0 / math.sqrt(QK_DIM)
    queries = absorbed_query.reshape(REQS, DRAFTS, HEADS, LATENT + ROPE)
    fresh_all = new_key.reshape(REQS, DRAFTS, LATENT + ROPE)

    def attend(packed):
        query_block, cache_rows, length, fresh_keys = packed
        query_wide = query_block.astype(jnp.float32)
        cache_wide = cache_rows.astype(jnp.float32)
        fresh_wide = fresh_keys.astype(jnp.float32)
        cache_scores = jnp.einsum('jhk,pk->jhp', query_wide, cache_wide) * score_scale
        live_mask = jnp.arange(CACHE, dtype=jnp.int32) < length
        cache_scores = jnp.where(live_mask[None, None, :], cache_scores, -1e+30)
        fresh_scores = jnp.einsum('jhk,ik->jhi', query_wide, fresh_wide) * score_scale
        causal = jnp.arange(DRAFTS, dtype=jnp.int32)[None, :] <= jnp.arange(DRAFTS, dtype=jnp.int32)[:, None]
        fresh_scores = jnp.where(causal[:, None, :], fresh_scores, -1e+30)
        peak = jnp.maximum(lax.optimization_barrier(jnp.max(cache_scores, axis=-1)), lax.optimization_barrier(jnp.max(fresh_scores, axis=-1)))[..., None]
        cache_expo = jnp.exp(cache_scores - peak)
        fresh_expo = jnp.exp(fresh_scores - peak)
        denom = lax.optimization_barrier(jnp.sum(cache_expo, axis=-1)) + lax.optimization_barrier(jnp.sum(fresh_expo, axis=-1))
        cache_probs = lax.optimization_barrier(cache_expo.astype(jnp.bfloat16)).astype(jnp.float32)
        fresh_probs = lax.optimization_barrier(fresh_expo.astype(jnp.bfloat16)).astype(jnp.float32)
        mixed_values = jnp.einsum('jhp,pl->jhl', cache_probs, cache_wide[:, :LATENT]) + jnp.einsum('jhi,il->jhl', fresh_probs, fresh_wide[:, :LATENT])
        return (mixed_values / denom[..., None]).astype(jnp.bfloat16)
    latent_attention = lax.map(attend, (queries, latent_cache, cache_length, fresh_all)).reshape(ROWS, HEADS, LATENT)
    slot_count = N_EP * N_DP * CAP
    pieces = N_TP * N_DP
    piece_width = FF_EXP // pieces

    def expert_step(running, packed):
        expert_index, gate_w, up_w, down_w = packed
        chosen = expert_ids == expert_index
        routed = jnp.any(chosen, axis=1)
        place_index = jnp.cumsum(routed.astype(jnp.int32)) - 1
        target = jnp.where(routed, place_index, slot_count)
        buffer = jnp.zeros((slot_count, D), jnp.bfloat16).at[target].set(projected, mode='drop')
        gate_out = jnp.dot(buffer, gate_w, preferred_element_type=jnp.float32)
        up_out = jnp.dot(buffer, up_w, preferred_element_type=jnp.float32)
        activated = (jax.nn.silu(gate_out) * up_out).astype(jnp.bfloat16)
        act_pieces = activated.reshape(slot_count, pieces, piece_width).astype(jnp.float32)
        down_pieces = down_w.reshape(pieces, piece_width, D).astype(jnp.float32)
        piece_sums = jnp.einsum('cqf,qfm->qcm', act_pieces, down_pieces)
        rounded = lax.optimization_barrier(piece_sums.astype(jnp.bfloat16)).astype(jnp.float32)
        result = lax.optimization_barrier(jnp.sum(rounded, axis=0)).astype(jnp.bfloat16)
        picked = result[jnp.clip(place_index, 0, slot_count - 1)].astype(jnp.float32)
        weight = lax.optimization_barrier(jnp.sum(jnp.where(chosen, gate_weights, 0.0), axis=1))
        return (running + weight[:, None] * picked, None)
    running, unused = lax.scan(expert_step, jnp.zeros((ROWS, D), jnp.float32), (jnp.arange(EXPERTS, dtype=jnp.int32), w_gate, w_up, w_down))
    return (latent_attention, running.astype(jnp.bfloat16))
```

```python
import math

import jax
import jax.numpy as jnp
from jax import lax
from jax.sharding import PartitionSpec as P

LATENT = 512
QK_DIM = 192


EPS = 1e-06


def rms_scale(values, gain_vector):
    wide = values.astype(jnp.float32)
    mean_square = jnp.mean(wide * wide, axis=-1, keepdims=True)
    return (wide * lax.rsqrt(mean_square + EPS) * gain_vector).astype(jnp.bfloat16)


def body(
    hidden,
    embedded,
    hidden_gain,
    embed_gain,
    w_embed,
    w_hidden,
    w_latent,
    latent_gain,
    absorbed_query,
    latent_cache,
    cache_length,
    expert_ids,
    gate_weights,
    w_gate,
    w_up,
    w_down,
):
    first_part = rms_scale(embedded, embed_gain)
    second_part = rms_scale(hidden, hidden_gain)
    embed_cols, hidden_cols = (
        lax.all_to_all(first_part, ("ep", "dp"), split_axis=1, concat_axis=0, tiled=True),
        lax.all_to_all(second_part, ("ep", "dp"), split_axis=1, concat_axis=0, tiled=True),
    )
    projected = lax.psum_scatter(
        (
            jnp.dot(embed_cols, w_embed, preferred_element_type=jnp.float32)
            + jnp.dot(hidden_cols, w_hidden, preferred_element_type=jnp.float32)
        ).astype(jnp.bfloat16),
        ("ep", "dp"),
        scatter_dimension=0,
        tiled=True,
    )
    latent_part = jnp.dot(projected, w_latent, preferred_element_type=jnp.float32)
    latent_full = lax.psum(latent_part.astype(jnp.bfloat16), "tp").astype(jnp.float32)
    new_key = jnp.concatenate(
        [
            rms_scale(latent_full[:, :LATENT], latent_gain),
            latent_full[:, LATENT:].astype(jnp.bfloat16),
        ],
        axis=1,
    )
    request_count = latent_cache.shape[0]
    row_count = projected.shape[0]
    draft_count = row_count // request_count
    head_count = absorbed_query.shape[1]
    key_width = absorbed_query.shape[2]
    cache_span = latent_cache.shape[1]
    score_scale = 1.0 / math.sqrt(QK_DIM)
    queries = absorbed_query.reshape(request_count, draft_count, head_count, key_width)
    fresh_keys = new_key.reshape(request_count, draft_count, key_width)
    cache_scores = (
        jnp.einsum("rjhk,rpk->rjhp", queries, latent_cache, preferred_element_type=jnp.float32)
        * score_scale
    )
    live_mask = jnp.arange(cache_span, dtype=jnp.int32)[None, :] < cache_length[:, None]
    cache_scores = jnp.where(live_mask[:, None, None, :], cache_scores, -1e30)
    fresh_scores = (
        jnp.einsum("rjhk,rik->rjhi", queries, fresh_keys, preferred_element_type=jnp.float32)
        * score_scale
    )
    causal = (
        jnp.arange(draft_count, dtype=jnp.int32)[None, :]
        <= jnp.arange(draft_count, dtype=jnp.int32)[:, None]
    )
    fresh_scores = jnp.where(causal[None, :, None, :], fresh_scores, -1e30)
    peak = jnp.maximum(jnp.max(cache_scores, axis=-1), jnp.max(fresh_scores, axis=-1))[..., None]
    cache_expo = jnp.exp(cache_scores - peak)
    fresh_expo = jnp.exp(fresh_scores - peak)
    denom = jnp.sum(cache_expo, axis=-1) + jnp.sum(fresh_expo, axis=-1)
    mixed_values = jnp.einsum(
        "rjhp,rpl->rjhl",
        cache_expo.astype(jnp.bfloat16),
        latent_cache[:, :, :LATENT],
        preferred_element_type=jnp.float32,
    )
    mixed_values = mixed_values + jnp.einsum(
        "rjhi,ril->rjhl",
        fresh_expo.astype(jnp.bfloat16),
        fresh_keys[:, :, :LATENT],
        preferred_element_type=jnp.float32,
    )
    latent_attention = (
        (mixed_values / denom[..., None])
        .astype(jnp.bfloat16)
        .reshape(row_count, head_count, LATENT)
    )
    local_experts = w_gate.shape[0]
    expert_count = local_experts * lax.axis_size("ep")
    chosen = expert_ids[:, :, None] == jnp.arange(expert_count, dtype=jnp.int32)
    row_weights = jnp.sum(jnp.where(chosen, gate_weights[:, :, None], 0.0), axis=1)
    all_weights = lax.all_gather(row_weights, ("ep", "dp"), axis=0, tiled=True)
    own_weights = lax.dynamic_slice_in_dim(
        all_weights, lax.axis_index("ep") * local_experts, local_experts, axis=1
    )
    features = lax.all_gather(projected, ("ep", "dp"), axis=0, tiled=True)
    features = lax.all_gather(features, "tp", axis=1, tiled=True)
    gate_out = jnp.einsum("rm,emf->erf", features, w_gate, preferred_element_type=jnp.float32)
    up_out = jnp.einsum("rm,emf->erf", features, w_up, preferred_element_type=jnp.float32)
    activated = (jax.nn.silu(gate_out) * up_out * own_weights.T[:, :, None]).astype(jnp.bfloat16)
    terms = jnp.einsum("erf,efm->rm", activated, w_down, preferred_element_type=jnp.float32)
    expert_mix = lax.psum_scatter(
        terms.astype(jnp.bfloat16), "tp", scatter_dimension=1, tiled=True
    )
    expert_mix = lax.psum_scatter(expert_mix, ("ep", "dp"), scatter_dimension=0, tiled=True)
    return (latent_attention, expert_mix)


def solution(mesh):
    placed = (
        P(("group", "ep", "dp"), None),
        P(("group", "ep", "dp"), None),
        P(),
        P(),
        P(("ep", "dp"), "tp"),
        P(("ep", "dp"), "tp"),
        P("tp", None),
        P(),
        P(("group", "ep", "dp"), "tp", None),
        P(("group", "ep", "dp"), None, None),
        P(("group", "ep", "dp")),
        P(("group", "ep", "dp"), None),
        P(("group", "ep", "dp"), None),
        P("ep", None, ("tp", "dp")),
        P("ep", None, ("tp", "dp")),
        P("ep", ("tp", "dp"), None),
    )
    return jax.shard_map(
        body,
        mesh=mesh,
        in_specs=placed,
        out_specs=(P(("group", "ep", "dp"), "tp", None), P(("group", "ep", "dp"), "tp")),
        check_vma=False,
    )
```

```python
import functools
import math

import jax
import jax.numpy as jnp
from jax import lax
from jax.experimental import pallas as pl
from jax.experimental.pallas import tpu as pltpu
from jax.sharding import PartitionSpec as P

LATENT = 512
QK_DIM = 192


EPS = 1e-06


def rms_scale(values, gain_vector):
    wide = values.astype(jnp.float32)
    mean_square = jnp.mean(wide * wide, axis=-1, keepdims=True)
    return (wide * lax.rsqrt(mean_square + EPS) * gain_vector).astype(jnp.bfloat16)


TILE = 512
MESH = pl.DeviceIdType.MESH


def step_kernel(
    n_ep,
    hidden,
    embedded,
    hidden_gain,
    embed_gain,
    weights_in,
    we_hbm,
    wh_hbm,
    wl_hbm,
    wg_hbm,
    wu_hbm,
    wd_hbm,
    mix_out,
    latent_out,
    w_area,
    wg,
    wu,
    wd_last,
    wl,
    x_send,
    x_recv,
    c_recv,
    p_send,
    p_one,
    p_sum,
    p_two,
    feats,
    act,
    o_send,
    o_one,
    o_sum,
    o_two,
    o_tot,
    o_three,
    l_send,
    l_recv,
    w_sem,
    g_sem,
    u_sem,
    d_sem,
    xs,
    xr,
    cs,
    cr,
    ps,
    pr,
    qs,
    qr,
    zs,
    zr,
    ts,
    tr,
    ss,
    sr,
    ys,
    yr,
    ls,
    lr,
    os1,
    or1,
    os2,
    or2,
    os3,
    or3,
):
    grp = lax.axis_index("group")
    e = lax.axis_index("ep")
    t = lax.axis_index("tp")
    d = lax.axis_index("dp")
    n_all = 2 * n_ep
    me = e * 2 + d
    depth = we_hbm.shape[0]
    half = we_hbm.shape[1]
    experts = wg_hbm.shape[0]
    ff = wg_hbm.shape[2]
    rows = hidden.shape[0]

    def at_row(n):
        return (grp, n // 2, t, lax.rem(n, 2))

    sibling = (grp, e, t, 1 - d)
    across = (grp, e, 1 - t, d)

    def ring(k):
        return lax.rem(e + k, n_ep)

    def back(k):
        return lax.rem(e + n_ep - k, n_ep)

    def on_ep(k):
        return (grp, ring(k), t, d)

    def send(src, dst, s_sem, r_sem, to):
        copy = pltpu.make_async_remote_copy(
            src_ref=src,
            dst_ref=dst,
            send_sem=s_sem,
            recv_sem=r_sem,
            device_id=to,
            device_id_type=MESH,
        )
        copy.start()
        return copy

    def wide(value):
        return value.astype(jnp.float32)

    barrier = pltpu.get_barrier_semaphore()
    for k in range(1, n_all):
        pl.semaphore_signal(
            barrier, inc=1, device_id=at_row(lax.rem(me + k, n_all)), device_id_type=MESH
        )
    pl.semaphore_signal(barrier, inc=1, device_id=across, device_id_type=MESH)

    we_copy = pltpu.make_async_copy(we_hbm, w_area.at[pl.ds(0, depth)], w_sem.at[0])
    wh_copy = pltpu.make_async_copy(wh_hbm, w_area.at[pl.ds(depth, depth)], w_sem.at[1])
    wl_copy = pltpu.make_async_copy(wl_hbm, wl, w_sem.at[2])
    we_copy.start()
    wh_copy.start()

    for part, (rows_in, gain) in enumerate(((embedded, embed_gain), (hidden, hidden_gain))):
        values = wide(rows_in[...])
        mean_square = jnp.mean(values * values, axis=-1, keepdims=True)
        scaled = (values * lax.rsqrt(mean_square + EPS) * gain[...]).astype(jnp.bfloat16)
        for n in range(n_all):
            x_send[n, part] = scaled[:, n * depth : (n + 1) * depth]

    pl.semaphore_wait(barrier, n_all)

    x_copies = []
    c_copies = []
    for k in range(1, n_all):
        n = lax.rem(me + k, n_all)
        x_copies.append(send(x_send.at[n], x_recv.at[me], xs.at[k], xr.at[k], at_row(n)))
    for k in range(1, n_all):
        n = lax.rem(me + k, n_all)
        c_copies.append(
            send(weights_in.at[n // 2], c_recv.at[me], cs.at[k], cr.at[k], at_row(n))
        )
    x_recv[me] = x_send[me]
    c_recv[me] = weights_in[e]

    wl_copy.start()

    def expert_copies(i):
        return (
            pltpu.make_async_copy(wg_hbm.at[i], wg.at[i], g_sem.at[i]),
            pltpu.make_async_copy(wu_hbm.at[i], wu.at[i], u_sem.at[i]),
        )

    for i in range(experts):
        for copy in expert_copies(i):
            copy.start()

    we_copy.wait()
    wh_copy.wait()
    for copy in x_copies:
        copy.wait_recv()

    embed_cols = x_recv[:, 0].reshape(n_all * rows, depth)
    hidden_cols = x_recv[:, 1].reshape(n_all * rows, depth)

    def project(j, carry):
        cols = pl.ds(pl.multiple_of(j * TILE, TILE), TILE)
        total = jnp.dot(
            embed_cols, w_area[pl.ds(0, depth), cols], preferred_element_type=jnp.float32
        ) + jnp.dot(
            hidden_cols, w_area[pl.ds(depth, depth), cols], preferred_element_type=jnp.float32
        )
        p_send[:, :, cols] = total.astype(jnp.bfloat16).reshape(n_all, rows, TILE)
        return carry

    lax.fori_loop(0, half // TILE, project, 0)

    order = list(range(1, n_ep)) + [0]
    p_first = {}
    for k in order:
        p_first[k] = send(
            p_send.at[ring(k) * 2 + 1 - d], p_one.at[k], ps.at[k], pr.at[k], sibling
        )

    mine = pl.ds(pl.multiple_of(t * half, half), half)
    other = pl.ds(pl.multiple_of((1 - t) * half, half), half)
    own_down = []
    other_down = []
    for i in range(experts):
        last = i == experts - 1
        target = wd_last if last else w_area.at[pl.ds((experts + i) * ff, ff)]
        copy = pltpu.make_async_copy(wd_hbm.at[i, :, other], target, d_sem.at[experts + i])
        copy.start()
        other_down.append(copy)
    for i in range(experts):
        copy = pltpu.make_async_copy(
            wd_hbm.at[i, :, mine], w_area.at[pl.ds(i * ff, ff)], d_sem.at[i]
        )
        copy.start()
        own_down.append(copy)

    p_second = {}
    for k in order:
        p_first[k].wait_recv()
        pair = wide(p_send[ring(k) * 2 + d]) + wide(p_one[k])
        if k:
            p_sum[k] = pair.astype(jnp.bfloat16)
            p_second[k] = send(p_sum.at[k], p_two.at[k], qs.at[k], qr.at[k], on_ep(k))
        else:
            total = pair
    for k in range(1, n_ep):
        p_second[k].wait_recv()
        total = total + wide(p_two[k])
    own = total.astype(jnp.bfloat16)
    feats[t, me] = own

    spread = {}
    sides = {}
    pairs = {}
    turned = {}
    block = feats.at[t, me]
    for k in range(1, n_ep):
        spread[k] = send(block, block, zs.at[k], zr.at[k], on_ep(k))
    sides[0] = send(block, block, ts.at[0], tr.at[0], across)
    pairs[0] = send(block, block, ss.at[0], sr.at[0], sibling)

    wl_copy.wait()
    l_send[...] = jnp.dot(own, wl[...], preferred_element_type=jnp.float32).astype(jnp.bfloat16)
    l_copy = send(l_send, l_recv, ls, lr, across)

    def turn(k):
        sides[k].wait_recv()
        there = feats.at[1 - t, back(k) * 2 + d]
        turned[k] = send(there, there, ys.at[k], yr.at[k], sibling)

    for k in range(1, n_ep):
        spread[k].wait_recv()
        here = feats.at[t, back(k) * 2 + d]
        sides[k] = send(here, here, ts.at[k], tr.at[k], across)
        pairs[k] = send(here, here, ss.at[k], sr.at[k], sibling)
        turn(k - 1)
    turn(n_ep - 1)
    l_copy.wait_recv()
    latent_out[...] = wide(l_send[...]) + wide(l_recv[...])
    for copy in c_copies:
        copy.wait_recv()
    for k in range(n_ep):
        pairs[k].wait_recv()
        turned[k].wait_recv()

    row_weights = c_recv[...].reshape(n_all * rows, c_recv.shape[2])
    lanes = lax.broadcasted_iota(jnp.int32, row_weights.shape, 1)

    def expert(i, carry):
        for copy in expert_copies(i):
            copy.wait()
        gate = jnp.zeros((n_all * rows, ff), jnp.float32)
        up = jnp.zeros((n_all * rows, ff), jnp.float32)
        for h in range(2):
            part = feats[h].reshape(n_all * rows, half)
            gate = gate + jnp.dot(
                part, wg[i, h * half : (h + 1) * half], preferred_element_type=jnp.float32
            )
            up = up + jnp.dot(
                part, wu[i, h * half : (h + 1) * half], preferred_element_type=jnp.float32
            )
        weight = jnp.sum(jnp.where(lanes == i, row_weights, 0.0), axis=1, keepdims=True)
        act[i] = (gate / (1.0 + jnp.exp(-gate)) * up * weight).astype(jnp.bfloat16)
        return carry

    lax.fori_loop(0, experts, expert, 0)

    def down(h, pieces):
        def tile(j, carry):
            cols = pl.ds(pl.multiple_of(j * TILE, TILE), TILE)
            total = jnp.zeros((n_all * rows, TILE), jnp.float32)
            for i, (ref, start) in enumerate(pieces):
                total = total + jnp.dot(
                    act[i], ref[pl.ds(start, ff), cols], preferred_element_type=jnp.float32
                )
            o_send[h, :, :, cols] = total.astype(jnp.bfloat16).reshape(n_all, rows, TILE)
            return carry

        lax.fori_loop(0, half // TILE, tile, 0)

    o_first = {}

    def exchange(h):
        for k in order:
            o_first[h, k] = send(
                o_send.at[h, ring(k) * 2 + 1 - d],
                o_one.at[h, k],
                os1.at[h, k],
                or1.at[h, k],
                sibling,
            )

    for copy in other_down:
        copy.wait()
    down(
        0,
        [(w_area, (experts + i) * ff) for i in range(experts - 1)] + [(wd_last, 0)],
    )
    exchange(0)
    o_second = {}
    for k in order:
        o_first[0, k].wait_recv()
        o_sum[k] = (wide(o_send[0, ring(k) * 2 + d]) + wide(o_one[0, k])).astype(jnp.bfloat16)
        o_second[k] = send(o_sum.at[k], o_two.at[k], os2.at[k], or2.at[k], across)
    for copy in own_down:
        copy.wait()
    down(1, [(w_area, i * ff) for i in range(experts)])
    exchange(1)
    o_third = {}
    for k in order:
        o_first[1, k].wait_recv()
        o_second[k].wait_recv()
        total = wide(o_send[1, ring(k) * 2 + d]) + wide(o_one[1, k]) + wide(o_two[k])
        if k:
            o_tot[k] = total.astype(jnp.bfloat16)
            o_third[k] = send(o_tot.at[k], o_three.at[k], os3.at[k], or3.at[k], on_ep(k))
    for k in range(1, n_ep):
        o_third[k].wait_recv()
        total = total + wide(o_three[k])
    mix_out[...] = total.astype(jnp.bfloat16)

    for group_of in (p_first, p_second, spread, sides, pairs, turned, o_first, o_second, o_third):
        for copy in group_of.values():
            copy.wait_send()
    for copy in x_copies + c_copies + [l_copy]:
        copy.wait_send()


def fused_step(
    hidden,
    embedded,
    hidden_gain,
    embed_gain,
    row_weights,
    w_embed,
    w_hidden,
    w_latent,
    w_gate,
    w_up,
    w_down,
):
    n_ep = lax.axis_size("ep")
    n_all = 2 * n_ep
    rows, width = hidden.shape
    depth, half = w_embed.shape
    experts, _, ff = w_gate.shape
    key_width = w_latent.shape[1]
    bf = jnp.bfloat16
    vmem = pl.BlockSpec(memory_space=pltpu.VMEM)
    hbm = pl.BlockSpec(memory_space=pl.ANY)
    dma = pltpu.SemaphoreType.DMA
    lanes = 128
    lined = jnp.transpose(row_weights.reshape(rows, n_ep, experts), (1, 0, 2))
    lined = jnp.pad(lined, ((0, 0), (0, 0), (0, lanes - experts)))
    area = max(2 * depth, (2 * experts - 1) * ff)
    block = (rows, half)
    scratch = [
        pltpu.VMEM((area, half), bf),
        pltpu.VMEM((experts, width, ff), bf),
        pltpu.VMEM((experts, width, ff), bf),
        pltpu.VMEM((ff, half), bf),
        pltpu.VMEM((half, key_width), bf),
        pltpu.VMEM((n_all, 2, rows, depth), bf),
        pltpu.VMEM((n_all, 2, rows, depth), bf),
        pltpu.VMEM((n_all, rows, lanes), jnp.float32),
        pltpu.VMEM((n_all,) + block, bf),
        pltpu.VMEM((n_ep,) + block, bf),
        pltpu.VMEM((n_ep,) + block, bf),
        pltpu.VMEM((n_ep,) + block, bf),
        pltpu.VMEM((2, n_all) + block, bf),
        pltpu.VMEM((experts, n_all * rows, ff), bf),
        pltpu.VMEM((2, n_all) + block, bf),
        pltpu.VMEM((2, n_ep) + block, bf),
        pltpu.VMEM((n_ep,) + block, bf),
        pltpu.VMEM((n_ep,) + block, bf),
        pltpu.VMEM((n_ep,) + block, bf),
        pltpu.VMEM((n_ep,) + block, bf),
        pltpu.VMEM((rows, key_width), bf),
        pltpu.VMEM((rows, key_width), bf),
        dma((3,)),
        dma((experts,)),
        dma((experts,)),
        dma((2 * experts,)),
    ]
    scratch += [dma((n_all,))] * 4
    scratch += [dma((n_ep,))] * 12
    scratch += [dma, dma]
    scratch += [dma((2, n_ep))] * 2
    scratch += [dma((n_ep,))] * 4
    return pl.pallas_call(
        functools.partial(step_kernel, n_ep),
        out_shape=(
            jax.ShapeDtypeStruct((rows, half), bf),
            jax.ShapeDtypeStruct((rows, key_width), jnp.float32),
        ),
        in_specs=[vmem] * 5 + [hbm] * 6,
        out_specs=(vmem, vmem),
        scratch_shapes=scratch,
        compiler_params=pltpu.CompilerParams(
            collective_id=0, has_side_effects=True, vmem_limit_bytes=62 * 1024 * 1024
        ),
        name="draft_step",
    )(
        hidden,
        embedded,
        hidden_gain[None, :],
        embed_gain[None, :],
        lined,
        w_embed,
        w_hidden,
        w_latent,
        w_gate,
        w_up,
        w_down,
    )


def plain_step(
    hidden,
    embedded,
    hidden_gain,
    embed_gain,
    row_weights,
    w_embed,
    w_hidden,
    w_latent,
    w_gate,
    w_up,
    w_down,
):
    first_part = rms_scale(embedded, embed_gain)
    second_part = rms_scale(hidden, hidden_gain)
    embed_cols, hidden_cols = (
        lax.all_to_all(first_part, ("ep", "dp"), split_axis=1, concat_axis=0, tiled=True),
        lax.all_to_all(second_part, ("ep", "dp"), split_axis=1, concat_axis=0, tiled=True),
    )
    projected = lax.psum_scatter(
        (
            jnp.dot(embed_cols, w_embed, preferred_element_type=jnp.float32)
            + jnp.dot(hidden_cols, w_hidden, preferred_element_type=jnp.float32)
        ).astype(jnp.bfloat16),
        ("ep", "dp"),
        scatter_dimension=0,
        tiled=True,
    )
    latent_part = jnp.dot(projected, w_latent, preferred_element_type=jnp.float32)
    latent_full = lax.psum(latent_part.astype(jnp.bfloat16), "tp").astype(jnp.float32)
    local_experts = w_gate.shape[0]
    all_weights = lax.all_gather(row_weights, ("ep", "dp"), axis=0, tiled=True)
    own_weights = lax.dynamic_slice_in_dim(
        all_weights, lax.axis_index("ep") * local_experts, local_experts, axis=1
    )
    features = lax.all_gather(projected, ("ep", "dp"), axis=0, tiled=True)
    features = lax.all_gather(features, "tp", axis=1, tiled=True)
    gate_out = jnp.einsum("rm,emf->erf", features, w_gate, preferred_element_type=jnp.float32)
    up_out = jnp.einsum("rm,emf->erf", features, w_up, preferred_element_type=jnp.float32)
    activated = (jax.nn.silu(gate_out) * up_out * own_weights.T[:, :, None]).astype(jnp.bfloat16)
    terms = jnp.einsum("erf,efm->rm", activated, w_down, preferred_element_type=jnp.float32)
    expert_mix = lax.psum_scatter(
        terms.astype(jnp.bfloat16), "tp", scatter_dimension=1, tiled=True
    )
    expert_mix = lax.psum_scatter(expert_mix, ("ep", "dp"), scatter_dimension=0, tiled=True)
    return expert_mix, latent_full


def body(
    hidden,
    embedded,
    hidden_gain,
    embed_gain,
    w_embed,
    w_hidden,
    w_latent,
    latent_gain,
    absorbed_query,
    latent_cache,
    cache_length,
    expert_ids,
    gate_weights,
    w_gate,
    w_up,
    w_down,
):
    local_experts = w_gate.shape[0]
    expert_count = local_experts * lax.axis_size("ep")
    chosen = expert_ids[:, :, None] == jnp.arange(expert_count, dtype=jnp.int32)
    row_weights = jnp.sum(jnp.where(chosen, gate_weights[:, :, None], 0.0), axis=1)
    fits = (
        lax.axis_size("tp") == 2
        and lax.axis_size("dp") == 2
        and w_embed.shape[0] % 128 == 0
        and w_embed.shape[1] % TILE == 0
        and hidden.shape[0] % 16 == 0
    )
    step = fused_step if fits else plain_step
    expert_mix, latent_full = step(
        hidden,
        embedded,
        hidden_gain,
        embed_gain,
        row_weights,
        w_embed,
        w_hidden,
        w_latent,
        w_gate,
        w_up,
        w_down,
    )
    new_key = jnp.concatenate(
        [
            rms_scale(latent_full[:, :LATENT], latent_gain),
            latent_full[:, LATENT:].astype(jnp.bfloat16),
        ],
        axis=1,
    )
    request_count = latent_cache.shape[0]
    row_count = hidden.shape[0]
    draft_count = row_count // request_count
    head_count = absorbed_query.shape[1]
    key_width = absorbed_query.shape[2]
    cache_span = latent_cache.shape[1]
    score_scale = 1.0 / math.sqrt(QK_DIM)
    queries = absorbed_query.reshape(request_count, draft_count, head_count, key_width)
    fresh_keys = new_key.reshape(request_count, draft_count, key_width)
    cache_scores = (
        jnp.einsum("rjhk,rpk->rjhp", queries, latent_cache, preferred_element_type=jnp.float32)
        * score_scale
    )
    live_mask = jnp.arange(cache_span, dtype=jnp.int32)[None, :] < cache_length[:, None]
    cache_scores = jnp.where(live_mask[:, None, None, :], cache_scores, -1e30)
    fresh_scores = (
        jnp.einsum("rjhk,rik->rjhi", queries, fresh_keys, preferred_element_type=jnp.float32)
        * score_scale
    )
    causal = (
        jnp.arange(draft_count, dtype=jnp.int32)[None, :]
        <= jnp.arange(draft_count, dtype=jnp.int32)[:, None]
    )
    fresh_scores = jnp.where(causal[None, :, None, :], fresh_scores, -1e30)
    peak = jnp.maximum(jnp.max(cache_scores, axis=-1), jnp.max(fresh_scores, axis=-1))[..., None]
    cache_expo = jnp.exp(cache_scores - peak)
    fresh_expo = jnp.exp(fresh_scores - peak)
    denom = jnp.sum(cache_expo, axis=-1) + jnp.sum(fresh_expo, axis=-1)
    mixed_values = jnp.einsum(
        "rjhp,rpl->rjhl",
        cache_expo.astype(jnp.bfloat16),
        latent_cache[:, :, :LATENT],
        preferred_element_type=jnp.float32,
    )
    mixed_values = mixed_values + jnp.einsum(
        "rjhi,ril->rjhl",
        fresh_expo.astype(jnp.bfloat16),
        fresh_keys[:, :, :LATENT],
        preferred_element_type=jnp.float32,
    )
    latent_attention = (
        (mixed_values / denom[..., None])
        .astype(jnp.bfloat16)
        .reshape(row_count, head_count, LATENT)
    )
    return (latent_attention, expert_mix)


def solution(mesh):
    placed = (
        P(("group", "ep", "dp"), None),
        P(("group", "ep", "dp"), None),
        P(),
        P(),
        P(("ep", "dp"), "tp"),
        P(("ep", "dp"), "tp"),
        P("tp", None),
        P(),
        P(("group", "ep", "dp"), "tp", None),
        P(("group", "ep", "dp"), None, None),
        P(("group", "ep", "dp")),
        P(("group", "ep", "dp"), None),
        P(("group", "ep", "dp"), None),
        P("ep", None, ("tp", "dp")),
        P("ep", None, ("tp", "dp")),
        P("ep", ("tp", "dp"), None),
    )
    return jax.shard_map(
        body,
        mesh=mesh,
        in_specs=placed,
        out_specs=(P(("group", "ep", "dp"), "tp", None), P(("group", "ep", "dp"), "tp")),
        check_vma=False,
    )
```

```python
import functools
import math

import jax
import jax.numpy as jnp
from jax import lax
from jax.experimental import pallas as pl
from jax.experimental.pallas import tpu as pltpu
from jax.sharding import PartitionSpec as P

LATENT = 512
QK_DIM = 192


EPS = 1e-06


def rms_scale(values, gain_vector):
    wide = values.astype(jnp.float32)
    mean_square = jnp.mean(wide * wide, axis=-1, keepdims=True)
    return (wide * lax.rsqrt(mean_square + EPS) * gain_vector).astype(jnp.bfloat16)


TILE = 512
MESH = pl.DeviceIdType.MESH


def step_kernel(
    n_ep,
    hidden,
    embedded,
    hidden_gain,
    embed_gain,
    weights_in,
    we_hbm,
    wh_hbm,
    wl_hbm,
    wg_hbm,
    wu_hbm,
    wd_hbm,
    query_hbm,
    cache_hbm,
    bias,
    latent_gain,
    mix_out,
    attn_out,
    w_area,
    wg,
    wu,
    wd_last,
    wl,
    x_send,
    x_recv,
    c_recv,
    p_send,
    p_one,
    p_sum,
    p_two,
    feats,
    act,
    o_one,
    o_sum,
    o_two,
    o_three,
    l_send,
    l_recv,
    query,
    cache,
    level,
    gate_part,
    up_part,
    w_sem,
    g_sem,
    u_sem,
    d_sem,
    xs,
    xr,
    cs,
    cr,
    ps,
    pr,
    qs,
    qr,
    zs,
    zr,
    ts,
    tr,
    ss,
    sr,
    ys,
    yr,
    ls,
    lr,
    os1,
    or1,
    os2,
    or2,
    os3,
    or3,
):
    grp = lax.axis_index("group")
    e = lax.axis_index("ep")
    t = lax.axis_index("tp")
    d = lax.axis_index("dp")
    n_all = 2 * n_ep
    me = e * 2 + d
    depth = we_hbm.shape[0]
    half = we_hbm.shape[1]
    experts = wg_hbm.shape[0]
    ff = wg_hbm.shape[2]
    rows = hidden.shape[0]

    def at_row(n):
        return (grp, n // 2, t, lax.rem(n, 2))

    sibling = (grp, e, t, 1 - d)
    across = (grp, e, 1 - t, d)

    def ring(k):
        return lax.rem(e + k, n_ep)

    def back(k):
        return lax.rem(e + n_ep - k, n_ep)

    def on_ep(k):
        return (grp, ring(k), t, d)

    def send(src, dst, s_sem, r_sem, to):
        copy = pltpu.make_async_remote_copy(
            src_ref=src,
            dst_ref=dst,
            send_sem=s_sem,
            recv_sem=r_sem,
            device_id=to,
            device_id_type=MESH,
        )
        copy.start()
        return copy

    def wide(value):
        return value.astype(jnp.float32)

    barrier = pltpu.get_barrier_semaphore()
    for k in range(1, n_all):
        pl.semaphore_signal(
            barrier, inc=1, device_id=at_row(lax.rem(me + k, n_all)), device_id_type=MESH
        )
    pl.semaphore_signal(barrier, inc=1, device_id=across, device_id_type=MESH)

    we_copy = pltpu.make_async_copy(we_hbm, w_area.at[pl.ds(0, depth)], w_sem.at[0])
    wh_copy = pltpu.make_async_copy(wh_hbm, w_area.at[pl.ds(depth, depth)], w_sem.at[1])
    wl_copy = pltpu.make_async_copy(wl_hbm, wl, w_sem.at[2])
    we_copy.start()
    wh_copy.start()
    query_copy = pltpu.make_async_copy(query_hbm, query, w_sem.at[3])
    cache_copy = pltpu.make_async_copy(cache_hbm, cache, w_sem.at[4])
    query_copy.start()
    cache_copy.start()

    for part, (rows_in, gain) in enumerate(((embedded, embed_gain), (hidden, hidden_gain))):
        values = wide(rows_in[...])
        mean_square = jnp.mean(values * values, axis=-1, keepdims=True)
        scaled = (values * lax.rsqrt(mean_square + EPS) * gain[...]).astype(jnp.bfloat16)
        for n in range(n_all):
            x_send[n, part] = scaled[:, n * depth : (n + 1) * depth]

    pl.semaphore_wait(barrier, n_all)

    x_copies = []
    c_copies = []
    for k in range(1, n_all):
        n = lax.rem(me + k, n_all)
        x_copies.append(send(x_send.at[n], x_recv.at[me], xs.at[k], xr.at[k], at_row(n)))
    for k in range(1, n_all):
        n = lax.rem(me + k, n_all)
        c_copies.append(
            send(weights_in.at[n // 2], c_recv.at[me], cs.at[k], cr.at[k], at_row(n))
        )
    x_recv[me] = x_send[me]
    c_recv[me] = weights_in[e]

    wl_copy.start()

    def expert_copies(i):
        return (
            pltpu.make_async_copy(wg_hbm.at[i], wg.at[i], g_sem.at[i]),
            pltpu.make_async_copy(wu_hbm.at[i], wu.at[i], u_sem.at[i]),
        )

    for i in range(experts):
        for copy in expert_copies(i):
            copy.start()

    query_copy.wait()
    cache_copy.wait()
    score_scale = 1.0 / math.sqrt(QK_DIM)

    def cached(r, carry):
        scores = (
            jnp.dot(query[r], cache[r], preferred_element_type=jnp.float32) * score_scale
            + bias[r]
        )
        peak = jnp.max(scores, axis=-1, keepdims=True)
        expo = jnp.exp(scores - peak)
        denom = jnp.sum(expo, axis=-1, keepdims=True)
        mixed = lax.dot_general(
            expo.astype(jnp.bfloat16),
            cache[r, 0:LATENT],
            (((1,), (1,)), ((), ())),
            preferred_element_type=jnp.float32,
        )
        attn_out[r] = (mixed / denom).astype(jnp.bfloat16)
        level[r] = peak + jnp.log(denom)
        return carry

    lax.fori_loop(0, query.shape[0], cached, 0)

    we_copy.wait()
    wh_copy.wait()
    for copy in x_copies:
        copy.wait_recv()

    embed_cols = x_recv[:, 0].reshape(n_all * rows, depth)
    hidden_cols = x_recv[:, 1].reshape(n_all * rows, depth)

    def project(j, carry):
        cols = pl.ds(pl.multiple_of(j * TILE, TILE), TILE)
        total = jnp.dot(
            embed_cols, w_area[pl.ds(0, depth), cols], preferred_element_type=jnp.float32
        ) + jnp.dot(
            hidden_cols, w_area[pl.ds(depth, depth), cols], preferred_element_type=jnp.float32
        )
        p_send[:, :, cols] = total.astype(jnp.bfloat16).reshape(n_all, rows, TILE)
        return carry

    lax.fori_loop(0, half // TILE, project, 0)

    order = list(range(1, n_ep)) + [0]
    p_first = {}
    for k in order:
        p_first[k] = send(
            p_send.at[ring(k) * 2 + 1 - d], p_one.at[k], ps.at[k], pr.at[k], sibling
        )

    mine = pl.ds(pl.multiple_of(t * half, half), half)
    other = pl.ds(pl.multiple_of((1 - t) * half, half), half)
    own_down = []
    other_down = []
    for i in range(experts):
        last = i == experts - 1
        target = wd_last if last else w_area.at[pl.ds((experts + i) * ff, ff)]
        copy = pltpu.make_async_copy(wd_hbm.at[i, :, other], target, d_sem.at[experts + i])
        copy.start()
        other_down.append(copy)
    for i in range(experts):
        copy = pltpu.make_async_copy(
            wd_hbm.at[i, :, mine], w_area.at[pl.ds(i * ff, ff)], d_sem.at[i]
        )
        copy.start()
        own_down.append(copy)

    p_second = {}
    for k in order:
        p_first[k].wait_recv()
        pair = wide(p_send[ring(k) * 2 + d]) + wide(p_one[k])
        if k:
            p_sum[k] = pair.astype(jnp.bfloat16)
            p_second[k] = send(p_sum.at[k], p_two.at[k], qs.at[k], qr.at[k], on_ep(k))
        else:
            total = pair
    for k in range(1, n_ep):
        p_second[k].wait_recv()
        total = total + wide(p_two[k])
    own = total.astype(jnp.bfloat16)
    feats[t, me] = own

    spread = {}
    sides = {}
    pairs = {}
    turned = {}
    block = feats.at[t, me]
    for k in range(1, n_ep):
        spread[k] = send(block, block, zs.at[k], zr.at[k], on_ep(k))
    sides[0] = send(block, block, ts.at[0], tr.at[0], across)
    pairs[0] = send(block, block, ss.at[0], sr.at[0], sibling)

    wl_copy.wait()
    l_send[...] = lax.dot_general(
        own, wl[...], (((1,), (1,)), ((), ())), preferred_element_type=jnp.float32
    ).astype(jnp.bfloat16)
    l_copy = send(l_send, l_recv, ls, lr, across)

    def turn(k):
        sides[k].wait_recv()
        there = feats.at[1 - t, back(k) * 2 + d]
        turned[k] = send(there, there, ys.at[k], yr.at[k], sibling)

    for k in range(1, n_ep):
        spread[k].wait_recv()
        here = feats.at[t, back(k) * 2 + d]
        sides[k] = send(here, here, ts.at[k], tr.at[k], across)
        pairs[k] = send(here, here, ss.at[k], sr.at[k], sibling)
        turn(k - 1)
    for k in range(n_ep):
        pairs[k].wait_recv()

    def halves(h, i):
        part = feats[h].reshape(n_all * rows, half)
        span = pl.ds(pl.multiple_of(h * half, half), half)
        return (
            jnp.dot(part, wg[i, span], preferred_element_type=jnp.float32),
            jnp.dot(part, wu[i, span], preferred_element_type=jnp.float32),
        )

    def first_half(i, carry):
        for copy in expert_copies(i):
            copy.wait()
        gate_part[i], up_part[i] = halves(t, i)
        return carry

    lax.fori_loop(0, experts // 2, first_half, 0)
    turn(n_ep - 1)
    for copy in c_copies:
        copy.wait_recv()
    for k in range(n_ep):
        turned[k].wait_recv()

    row_weights = c_recv[...].reshape(n_all * rows, c_recv.shape[2])
    lanes = lax.broadcasted_iota(jnp.int32, row_weights.shape, 1)

    def finish(i, gate, up):
        weight = jnp.sum(jnp.where(lanes == i, row_weights, 0.0), axis=1, keepdims=True)
        act[i] = (gate / (1.0 + jnp.exp(-gate)) * up * weight).astype(jnp.bfloat16)

    def begun(i, carry):
        gate, up = halves(1 - t, i)
        finish(i, gate + gate_part[i], up + up_part[i])
        return carry

    def whole(i, carry):
        for copy in expert_copies(i):
            copy.wait()
        gate, up = halves(t, i)
        gate_rest, up_rest = halves(1 - t, i)
        finish(i, gate + gate_rest, up + up_rest)
        return carry

    lax.fori_loop(0, experts // 2, begun, 0)
    lax.fori_loop(experts // 2, experts, whole, 0)
    for group_of in (spread, sides, pairs, turned):
        for copy in group_of.values():
            copy.wait_send()
    o_send = feats

    def down(h, pieces):
        def tile(j, carry):
            cols = pl.ds(pl.multiple_of(j * TILE, TILE), TILE)
            total = jnp.zeros((n_all * rows, TILE), jnp.float32)
            for i, (ref, start) in enumerate(pieces):
                total = total + jnp.dot(
                    act[i], ref[pl.ds(start, ff), cols], preferred_element_type=jnp.float32
                )
            o_send[h, :, :, cols] = total.astype(jnp.bfloat16).reshape(n_all, rows, TILE)
            return carry

        lax.fori_loop(0, half // TILE, tile, 0)

    o_first = {}

    def exchange(h):
        for k in order:
            o_first[h, k] = send(
                o_send.at[h, ring(k) * 2 + 1 - d],
                o_one.at[h, k],
                os1.at[h, k],
                or1.at[h, k],
                sibling,
            )

    for copy in other_down:
        copy.wait()
    down(
        0,
        [(w_area, (experts + i) * ff) for i in range(experts - 1)] + [(wd_last, 0)],
    )
    exchange(0)
    o_second = {}
    for k in order:
        o_first[0, k].wait_recv()
        o_sum[k] = (wide(o_send[0, ring(k) * 2 + d]) + wide(o_one[0, k])).astype(jnp.bfloat16)
        o_second[k] = send(o_sum.at[k], o_two.at[k], os2.at[k], or2.at[k], across)
    for copy in own_down:
        copy.wait()
    down(1, [(w_area, i * ff) for i in range(experts)])
    exchange(1)
    o_third = {}
    for k in order:
        o_first[1, k].wait_recv()
        o_second[k].wait_recv()
        total = wide(o_send[1, ring(k) * 2 + d]) + wide(o_one[1, k]) + wide(o_two[k])
        if k:
            p_second[k].wait_send()
            p_sum[k] = total.astype(jnp.bfloat16)
            o_third[k] = send(p_sum.at[k], o_three.at[k], os3.at[k], or3.at[k], on_ep(k))
    l_copy.wait_recv()
    latent_full = wide(l_send[...]) + wide(l_recv[...])
    latent = latent_full[:, :LATENT]
    mean_square = jnp.mean(latent * latent, axis=-1, keepdims=True)
    fresh_values = (latent * lax.rsqrt(mean_square + EPS) * latent_gain[...]).astype(jnp.bfloat16)
    fresh_rope = latent_full[:, LATENT:].astype(jnp.bfloat16)
    requests, pairs_of, _ = query.shape
    drafts = rows // requests
    heads = pairs_of // drafts
    key_at = lax.broadcasted_iota(jnp.int32, (pairs_of, rows), 1)
    pair_at = lax.broadcasted_iota(jnp.int32, (pairs_of, rows), 0)

    def fresh(r, carry):
        turned_dims = (((1,), (1,)), ((), ()))
        scores = score_scale * (
            lax.dot_general(
                query[r, :, 0:LATENT], fresh_values, turned_dims, preferred_element_type=jnp.float32
            )
            + lax.dot_general(
                query[r, :, LATENT:], fresh_rope, turned_dims, preferred_element_type=jnp.float32
            )
        )
        draft = key_at - r * drafts
        seen = (draft >= 0) & (draft * heads <= pair_at)
        scores = jnp.where(seen, scores, -1e30)
        peak = jnp.maximum(level[r], jnp.max(scores, axis=-1, keepdims=True))
        expo = jnp.exp(scores - peak)
        share = jnp.exp(level[r] - peak)
        denom = share + jnp.sum(expo, axis=-1, keepdims=True)
        mixed = wide(attn_out[r]) * share + jnp.dot(
            expo.astype(jnp.bfloat16), fresh_values, preferred_element_type=jnp.float32
        )
        attn_out[r] = (mixed / denom).astype(jnp.bfloat16)
        return carry

    lax.fori_loop(0, requests, fresh, 0)

    for k in range(1, n_ep):
        o_third[k].wait_recv()
        total = total + wide(o_three[k])
    mix_out[...] = total.astype(jnp.bfloat16)

    for group_of in (p_first, o_first, o_second, o_third):
        for copy in group_of.values():
            copy.wait_send()
    for copy in x_copies + c_copies + [l_copy]:
        copy.wait_send()


def fused_step(
    hidden,
    embedded,
    hidden_gain,
    embed_gain,
    row_weights,
    w_embed,
    w_hidden,
    w_latent,
    w_gate,
    w_up,
    w_down,
    absorbed_query,
    latent_cache,
    cache_length,
    latent_gain,
):
    n_ep = lax.axis_size("ep")
    n_all = 2 * n_ep
    rows, width = hidden.shape
    depth, half = w_embed.shape
    experts, _, ff = w_gate.shape
    key_width = w_latent.shape[1]
    bf = jnp.bfloat16
    requests, span, _ = latent_cache.shape
    heads = absorbed_query.shape[1]
    pairs_of = rows // requests * heads
    live = jnp.arange(span, dtype=jnp.int32)[None, :] < cache_length[:, None]
    bias = jnp.where(live, 0.0, -1e30).astype(jnp.float32)[:, None, :]
    vmem = pl.BlockSpec(memory_space=pltpu.VMEM)
    hbm = pl.BlockSpec(memory_space=pl.ANY)
    dma = pltpu.SemaphoreType.DMA
    lanes = 128
    lined = jnp.transpose(row_weights.reshape(rows, n_ep, experts), (1, 0, 2))
    lined = jnp.pad(lined, ((0, 0), (0, 0), (0, lanes - experts)))
    area = max(2 * depth, (2 * experts - 1) * ff)
    block = (rows, half)
    scratch = [
        pltpu.VMEM((area, half), bf),
        pltpu.VMEM((experts, width, ff), bf),
        pltpu.VMEM((experts, width, ff), bf),
        pltpu.VMEM((ff, half), bf),
        pltpu.VMEM((key_width, half), bf),
        pltpu.VMEM((n_all, 2, rows, depth), bf),
        pltpu.VMEM((n_all, 2, rows, depth), bf),
        pltpu.VMEM((n_all, rows, lanes), jnp.float32),
        pltpu.VMEM((n_all,) + block, bf),
        pltpu.VMEM((n_ep,) + block, bf),
        pltpu.VMEM((n_ep,) + block, bf),
        pltpu.VMEM((n_ep,) + block, bf),
        pltpu.VMEM((2, n_all) + block, bf),
        pltpu.VMEM((experts, n_all * rows, ff), bf),
        pltpu.VMEM((2, n_ep) + block, bf),
        pltpu.VMEM((n_ep,) + block, bf),
        pltpu.VMEM((n_ep,) + block, bf),
        pltpu.VMEM((n_ep,) + block, bf),
        pltpu.VMEM((rows, key_width), bf),
        pltpu.VMEM((rows, key_width), bf),
        pltpu.VMEM((requests, pairs_of, key_width), bf),
        pltpu.VMEM((requests, key_width, span), bf),
        pltpu.VMEM((requests, pairs_of, 1), jnp.float32),
        pltpu.VMEM((experts // 2, n_all * rows, ff), jnp.float32),
        pltpu.VMEM((experts // 2, n_all * rows, ff), jnp.float32),
        dma((5,)),
        dma((experts,)),
        dma((experts,)),
        dma((2 * experts,)),
    ]
    scratch += [dma((n_all,))] * 4
    scratch += [dma((n_ep,))] * 12
    scratch += [dma, dma]
    scratch += [dma((2, n_ep))] * 2
    scratch += [dma((n_ep,))] * 4
    mix, attention = pl.pallas_call(
        functools.partial(step_kernel, n_ep),
        out_shape=(
            jax.ShapeDtypeStruct((rows, half), bf),
            jax.ShapeDtypeStruct((requests, pairs_of, LATENT), bf),
        ),
        in_specs=[vmem] * 5 + [hbm] * 8 + [vmem] * 2,
        out_specs=(vmem, vmem),
        scratch_shapes=scratch,
        compiler_params=pltpu.CompilerParams(
            collective_id=0, has_side_effects=True, vmem_limit_bytes=127 * 512 * 1024
        ),
        name="draft_step",
    )(
        hidden,
        embedded,
        hidden_gain[None, :],
        embed_gain[None, :],
        lined,
        w_embed,
        w_hidden,
        jnp.swapaxes(w_latent, 0, 1),
        w_gate,
        w_up,
        w_down,
        absorbed_query.reshape(requests, pairs_of, key_width),
        jnp.swapaxes(latent_cache, 1, 2),
        bias,
        latent_gain[None, :],
    )
    return attention.reshape(rows, heads, LATENT), mix


def plain_step(
    hidden,
    embedded,
    hidden_gain,
    embed_gain,
    row_weights,
    w_embed,
    w_hidden,
    w_latent,
    w_gate,
    w_up,
    w_down,
):
    first_part = rms_scale(embedded, embed_gain)
    second_part = rms_scale(hidden, hidden_gain)
    embed_cols, hidden_cols = (
        lax.all_to_all(first_part, ("ep", "dp"), split_axis=1, concat_axis=0, tiled=True),
        lax.all_to_all(second_part, ("ep", "dp"), split_axis=1, concat_axis=0, tiled=True),
    )
    projected = lax.psum_scatter(
        (
            jnp.dot(embed_cols, w_embed, preferred_element_type=jnp.float32)
            + jnp.dot(hidden_cols, w_hidden, preferred_element_type=jnp.float32)
        ).astype(jnp.bfloat16),
        ("ep", "dp"),
        scatter_dimension=0,
        tiled=True,
    )
    latent_part = jnp.dot(projected, w_latent, preferred_element_type=jnp.float32)
    latent_full = lax.psum(latent_part.astype(jnp.bfloat16), "tp").astype(jnp.float32)
    local_experts = w_gate.shape[0]
    all_weights = lax.all_gather(row_weights, ("ep", "dp"), axis=0, tiled=True)
    own_weights = lax.dynamic_slice_in_dim(
        all_weights, lax.axis_index("ep") * local_experts, local_experts, axis=1
    )
    features = lax.all_gather(projected, ("ep", "dp"), axis=0, tiled=True)
    features = lax.all_gather(features, "tp", axis=1, tiled=True)
    gate_out = jnp.einsum("rm,emf->erf", features, w_gate, preferred_element_type=jnp.float32)
    up_out = jnp.einsum("rm,emf->erf", features, w_up, preferred_element_type=jnp.float32)
    activated = (jax.nn.silu(gate_out) * up_out * own_weights.T[:, :, None]).astype(jnp.bfloat16)
    terms = jnp.einsum("erf,efm->rm", activated, w_down, preferred_element_type=jnp.float32)
    expert_mix = lax.psum_scatter(
        terms.astype(jnp.bfloat16), "tp", scatter_dimension=1, tiled=True
    )
    expert_mix = lax.psum_scatter(expert_mix, ("ep", "dp"), scatter_dimension=0, tiled=True)
    return expert_mix, latent_full


def body(
    hidden,
    embedded,
    hidden_gain,
    embed_gain,
    w_embed,
    w_hidden,
    w_latent,
    latent_gain,
    absorbed_query,
    latent_cache,
    cache_length,
    expert_ids,
    gate_weights,
    w_gate,
    w_up,
    w_down,
):
    local_experts = w_gate.shape[0]
    expert_count = local_experts * lax.axis_size("ep")
    chosen = expert_ids[:, :, None] == jnp.arange(expert_count, dtype=jnp.int32)
    row_weights = jnp.sum(jnp.where(chosen, gate_weights[:, :, None], 0.0), axis=1)
    fits = (
        lax.axis_size("tp") == 2
        and lax.axis_size("dp") == 2
        and w_embed.shape[0] % 128 == 0
        and w_embed.shape[1] % TILE == 0
        and hidden.shape[0] % 16 == 0
        and w_gate.shape[0] % 2 == 0
    )
    if fits:
        return fused_step(
            hidden,
            embedded,
            hidden_gain,
            embed_gain,
            row_weights,
            w_embed,
            w_hidden,
            w_latent,
            w_gate,
            w_up,
            w_down,
            absorbed_query,
            latent_cache,
            cache_length,
            latent_gain,
        )
    expert_mix, latent_full = plain_step(
        hidden,
        embedded,
        hidden_gain,
        embed_gain,
        row_weights,
        w_embed,
        w_hidden,
        w_latent,
        w_gate,
        w_up,
        w_down,
    )
    new_key = jnp.concatenate(
        [
            rms_scale(latent_full[:, :LATENT], latent_gain),
            latent_full[:, LATENT:].astype(jnp.bfloat16),
        ],
        axis=1,
    )
    request_count = latent_cache.shape[0]
    row_count = hidden.shape[0]
    draft_count = row_count // request_count
    head_count = absorbed_query.shape[1]
    key_width = absorbed_query.shape[2]
    cache_span = latent_cache.shape[1]
    score_scale = 1.0 / math.sqrt(QK_DIM)
    queries = absorbed_query.reshape(request_count, draft_count, head_count, key_width)
    fresh_keys = new_key.reshape(request_count, draft_count, key_width)
    cache_scores = (
        jnp.einsum("rjhk,rpk->rjhp", queries, latent_cache, preferred_element_type=jnp.float32)
        * score_scale
    )
    live_mask = jnp.arange(cache_span, dtype=jnp.int32)[None, :] < cache_length[:, None]
    cache_scores = jnp.where(live_mask[:, None, None, :], cache_scores, -1e30)
    fresh_scores = (
        jnp.einsum("rjhk,rik->rjhi", queries, fresh_keys, preferred_element_type=jnp.float32)
        * score_scale
    )
    causal = (
        jnp.arange(draft_count, dtype=jnp.int32)[None, :]
        <= jnp.arange(draft_count, dtype=jnp.int32)[:, None]
    )
    fresh_scores = jnp.where(causal[None, :, None, :], fresh_scores, -1e30)
    peak = jnp.maximum(jnp.max(cache_scores, axis=-1), jnp.max(fresh_scores, axis=-1))[..., None]
    cache_expo = jnp.exp(cache_scores - peak)
    fresh_expo = jnp.exp(fresh_scores - peak)
    denom = jnp.sum(cache_expo, axis=-1) + jnp.sum(fresh_expo, axis=-1)
    mixed_values = jnp.einsum(
        "rjhp,rpl->rjhl",
        cache_expo.astype(jnp.bfloat16),
        latent_cache[:, :, :LATENT],
        preferred_element_type=jnp.float32,
    )
    mixed_values = mixed_values + jnp.einsum(
        "rjhi,ril->rjhl",
        fresh_expo.astype(jnp.bfloat16),
        fresh_keys[:, :, :LATENT],
        preferred_element_type=jnp.float32,
    )
    latent_attention = (
        (mixed_values / denom[..., None])
        .astype(jnp.bfloat16)
        .reshape(row_count, head_count, LATENT)
    )
    return (latent_attention, expert_mix)


def solution(mesh):
    placed = (
        P(("group", "ep", "dp"), None),
        P(("group", "ep", "dp"), None),
        P(),
        P(),
        P(("ep", "dp"), "tp"),
        P(("ep", "dp"), "tp"),
        P("tp", None),
        P(),
        P(("group", "ep", "dp"), "tp", None),
        P(("group", "ep", "dp"), None, None),
        P(("group", "ep", "dp")),
        P(("group", "ep", "dp"), None),
        P(("group", "ep", "dp"), None),
        P("ep", None, ("tp", "dp")),
        P("ep", None, ("tp", "dp")),
        P("ep", ("tp", "dp"), None),
    )
    return jax.shard_map(
        body,
        mesh=mesh,
        in_specs=placed,
        out_specs=(P(("group", "ep", "dp"), "tp", None), P(("group", "ep", "dp"), "tp")),
        check_vma=False,
    )
```
